512 devices in a mesh: tm: 8 (over x, y_hi), tile: 64 (over z, y_lo, core).
Axes of the slice: x: 4, y: 4 (y_hi: 2, y_lo: 2; y = y_hi * 2 + y_lo), z: 16, core: 2. Of those that a mesh axis runs over, the one named last changes fastest.
Arguments:
- blocks: float32 [8, 320, 128, 128], P('tm', None, 'tile'), may hold values from -16 to 16
- coef_first: float32 [128, 128], P('tile'), may hold values from 0.5 to 2
- coef_second: float32 [128, 128], P('tile'), may hold values from 0.5 to 2
- wet: int32 [128, 128], P('tile'), may hold values 0 or 1
Outputs:
- hessian: float32 [8, 320, 320], P('tm', 'tile')
The draws below stay inside these ranges and needn't reach their ends.
All inputs are finite; a program needn't handle non-finite values. No bound on the sum of `wet` on one device may be relied on, other than what follows from the above.
Results may differ from the reference program's by a relative error of at most 0.000088.
Values sent between devices are 32-bit elements; how exact they have to be, the bound alone decides.
No kernel may reach another device: no remote copies, remote signals or barrier semaphores. Data moves between devices by JAX's collectives and lax.ppermute only.
A program may use at most 64 MiB of HBM per device.

```python
import math
import jax
import jax.numpy as jnp
from jax import lax

OBS = 320
COLS = 128
ROWS = 128
PARAMS = 16384
NDIAG = 8


def plant(entries, own_key, least, largest):
    index_at = [jax.random.randint(jax.random.fold_in(own_key, axis), (), 0, length) for axis, length in enumerate(entries.shape)]
    longest = entries.shape.index(max(entries.shape))
    next_to = index_at[:longest] + [(index_at[longest] + 1) % entries.shape[longest]] + index_at[longest + 1:]
    return entries.at[tuple(index_at)].set(least).at[tuple(next_to)].set(largest)


def strengthened(values, key, source, target, shards_of, factor):
    owner, partner = [(jnp.arange(values.shape[dim]) // (values.shape[dim] // shards_of)).reshape([-1 if axis == dim else 1 for axis in range(values.ndim)]) for dim in (source, target)]
    chosen = jax.random.permutation(key, shards_of)[partner]
    strong = (owner == chosen) | (owner == (partner + shards_of // 2) % shards_of)
    return jnp.where(strong, factor * values, values)


def shard_levels(own_key, dims, shards, least, high):
    gain = 1.0
    for axis_at, blocks in shards:
        heights = jax.random.uniform(jax.random.fold_in(jax.random.fold_in(own_key, 6), axis_at), (blocks,), jnp.float32, least / len(shards), high / len(shards))
        gain = gain * jnp.repeat(jnp.exp(heights), dims[axis_at] // blocks).reshape((-1,) + (1,) * (len(dims) - 1 - axis_at))
    return gain


def noise_with(own_key, shape, width, bound, cuts, heavy, kind=jnp.bfloat16):
    values = width * jax.random.normal(own_key, shape, jnp.float32)
    if cuts:
        values = values * shard_levels(own_key, shape, cuts, -0.22, 0.18)
    return jnp.clip(strengthened(values, jax.random.fold_in(own_key, 3), *heavy), -bound, bound).astype(kind)


def setup_inputs(seed: int = 0) -> dict:
    splits = jax.random.split(jax.random.key(seed), 5)
    blocks = noise_with(splits[0], (NDIAG, OBS, ROWS, COLS), 1.0, 16.0, ((0, 8), (2, 64)), (2, 1, 64, 4.0), jnp.float32)
    coef_first = jnp.clip(jnp.exp(math.log(2.0) - 1.3862944 * jax.random.uniform(splits[1], (ROWS, COLS), jnp.float32) ** shard_levels(splits[1], (ROWS, COLS), ((0, 64),), -0.2, 0.2)), 0.5, 2.0)
    coef_second = jnp.clip(jnp.exp(math.log(2.0) - 1.3862944 * jax.random.uniform(splits[2], (ROWS, COLS), jnp.float32) ** shard_levels(splits[2], (ROWS, COLS), ((0, 64),), -0.2, 0.2)), 0.5, 2.0)
    wet = plant((jax.random.randint(splits[3], (ROWS, COLS), 0, 5) < 4).astype(jnp.int32), jax.random.fold_in(splits[3], 1), 0, 1)
    return dict(blocks=blocks, coef_first=coef_first, coef_second=coef_second, wet=wet)


def sweep(field, coef, wetf):
    masked = field * wetf
    widths = ((0, 0),) * (masked.ndim - 2) + ((1, 1), (1, 1))
    padded = jnp.pad(masked, widths)
    beside = padded[..., 2:, 1:-1] + padded[..., :-2, 1:-1]
    beside = beside + padded[..., 1:-1, 2:] + padded[..., 1:-1, :-2]
    return coef * masked + 0.2 * beside


def reference(blocks, coef_first, coef_second, wet):
    wetf = wet.astype(jnp.float32)

    def smooth_one(block):
        return sweep(sweep(block, coef_first, wetf), coef_second, wetf)

    smooth = lax.map(smooth_one, blocks)
    flat = smooth.reshape(NDIAG, OBS, PARAMS)

    def diagonal(shift):
        partner = jnp.roll(flat, -shift, axis=0)
        return jnp.einsum("gop,gqp->oq", flat, partner, precision=lax.Precision.HIGHEST)

    shifts = jnp.arange(NDIAG, dtype=jnp.int32)
    total = lax.map(diagonal, shifts)
    return total / jnp.float32(PARAMS)
```

```python
import jax
import jax.numpy as jnp
from jax import lax
from jax.experimental import pallas as pl
from jax.experimental.pallas import tpu as pltpu
from jax.sharding import Mesh
from jax.sharding import PartitionSpec as P

TM = ("xh", "xl", "yh")
TILE = ("z", "yl", "c")
LAGS, OBS, COLS = 8, 320, 128
DEPTH, QUAD = 16, 4
MINE = OBS // (DEPTH * QUAD)
PACKED = 648

VM = pl.BlockSpec(memory_space=pltpu.VMEM)


def call(body, shape, args, scratch=(), limit=16, smem=0):
    specs = [VM] * len(args)
    for i in range(smem):
        specs[len(args) - 1 - i] = pl.BlockSpec(memory_space=pltpu.SMEM)
    return pl.pallas_call(
        body,
        out_shape=jax.ShapeDtypeStruct(shape, jnp.float32),
        in_specs=specs,
        out_specs=VM,
        scratch_shapes=list(scratch),
        compiler_params=pltpu.CompilerParams(vmem_limit_bytes=limit * 2**20),
    )(*args)


def pack_body(block_ref, coef_ref, second_ref, wet_ref, out_ref, wet_in, sems):
    copies = [
        pltpu.make_async_copy(src, to, sems.at[i])
        for i, (src, to) in enumerate(
            (
                (wet_ref, wet_in),
                (coef_ref, out_ref.at[2 * OBS : 2 * OBS + 2]),
                (second_ref, out_ref.at[2 * OBS + 4 : 2 * OBS + 6]),
                (block_ref, out_ref.at[0 : 2 * OBS]),
            )
        )
    ]
    for copy in copies:
        copy.start()
    for copy in copies:
        copy.wait()
    wet = wet_in[...].astype(jnp.float32)
    both = jnp.concatenate([wet] * 4, axis=0)
    for i in range(0, 2 * OBS, 8):
        out_ref[i : i + 8, :] = out_ref[i : i + 8, :] * both
    out_ref[2 * OBS + 2 : 2 * OBS + 4, :] = wet
    out_ref[2 * OBS + 6 :, :] = jnp.zeros((2, COLS), jnp.float32)


def smooth_body(own_ref, up_ref, down_ref, out_ref):
    lane = lax.broadcasted_iota(jnp.int32, (1, COLS), 1)
    fifth_l = jnp.where(lane > 0, 0.2, 0.0).astype(jnp.float32)
    fifth_r = jnp.where(lane < COLS - 1, 0.2, 0.0).astype(jnp.float32)

    def lateral(u):
        return pltpu.roll(u, 1, 1) * fifth_l + pltpu.roll(u, COLS - 1, 1) * fifth_r

    def row(ref, i):
        return ref[2 * OBS + i : 2 * OBS + i + 1, :]

    coef = [row(up_ref, 1), row(own_ref, 0), row(own_ref, 1), row(down_ref, 0)]
    wet = [row(up_ref, 3), row(own_ref, 2), row(own_ref, 3), row(down_ref, 2)]
    late = [row(own_ref, 4), row(own_ref, 5)]
    n = 32
    for o in range(0, OBS, n):
        rows = [
            ref[pl.ds(2 * o + r, n, 2), :]
            for ref in (up_ref, own_ref, down_ref)
            for r in (0, 1)
        ]
        first = []
        for i in range(4):
            mid = rows[i + 1]
            total = coef[i] * mid + 0.2 * (rows[i] + rows[i + 2]) + lateral(mid)
            first.append(total * wet[i])
        for r in range(2):
            mid = first[r + 1]
            value = late[r] * mid + 0.2 * (first[r] + first[r + 2]) + lateral(mid)
            for t in range(LAGS):
                if t // 2 % 2 == r:
                    out_ref[t, o : o + n, :] = value


def lag_body(all_ref, shift_ref, out_ref, hi_ref, lo_ref, acc_ref):
    for g in range(LAGS):
        full = all_ref[g]
        hi = full.astype(jnp.bfloat16)
        lo = (full - hi.astype(jnp.float32)).astype(jnp.bfloat16)
        before = (g + LAGS - 1) % LAGS
        for ref, value in ((hi_ref, hi), (lo_ref, lo)):
            ref[g, :, 0:COLS] = value
            ref[before, :, COLS : 2 * COLS] = value

    def product(a, b):
        return lax.dot_general(
            a, b, (((1,), (1,)), ((), ())), preferred_element_type=jnp.float32
        )

    half = DEPTH // 2 * MINE
    for pick in range(2):
        total = None
        for g in range(0, LAGS, 2):
            partner = lax.rem(shift_ref[0] + (2 * pick + g), LAGS)
            hi, lo = hi_ref[g], lo_ref[g]
            hi_p, lo_p = hi_ref[partner], lo_ref[partner]
            term = product(hi, hi_p) + (product(hi, lo_p) + product(lo, hi_p))
            total = term if total is None else total + term
        acc_ref[...] = total
        for q in range(QUAD):
            to_q = pick * QUAD + q
            for z in range(DEPTH):
                src = slice((z * QUAD + q) * MINE, (z * QUAD + q + 1) * MINE)
                to = z * MINE
                out_ref[to_q, to : to + MINE, :] = acc_ref[src, 0:128]
                out_ref[to_q, 2 * half + to : 2 * half + to + MINE, :] = acc_ref[src, 128:256]
                to, side = (to % half) + 4 * half, (to // half) * 64
                out_ref[to_q, to : to + MINE, side : side + 64] = acc_ref[src, 256:320]


def summed(parts):
    while len(parts) > 1:
        parts = [a + b for a, b in zip(parts[::2], parts[1::2])]
    return parts[0]


def quad_body(in_ref, out_ref):
    half = DEPTH // 2 * MINE
    total = summed([in_ref[i] for i in range(2 * QUAD)])
    left, mid, last = total[: 2 * half], total[2 * half : 4 * half], total[4 * half :]
    swapped = pltpu.roll(last, 64, 1)
    for z in range(DEPTH):
        to = z * MINE
        out_ref[z, 0:MINE, :] = left[to : to + MINE]
        out_ref[z, MINE : 2 * MINE, :] = mid[to : to + MINE]
        side = last if to < half else swapped
        out_ref[z, 2 * MINE : 3 * MINE, :] = side[to % half : to % half + MINE]
        out_ref[z, 3 * MINE :, :] = jnp.zeros((1, 128), jnp.float32)


def final_body(in_ref, out_ref):
    total = summed([in_ref[i] for i in range(DEPTH)]) * (1.0 / 16384.0)
    out_ref[:, 0, 0:128] = total[0:MINE]
    out_ref[:, 0, 128:256] = total[MINE : 2 * MINE]
    out_ref[:, 0, 256:320] = total[2 * MINE : 3 * MINE, 0:64]


def shards(blocks, coef_first, coef_second, wet):
    own = pl.pallas_call(
        pack_body,
        out_shape=jax.ShapeDtypeStruct((PACKED, COLS), jnp.float32),
        in_specs=[pl.BlockSpec(memory_space=pltpu.HBM)] * 4,
        out_specs=VM,
        scratch_shapes=[pltpu.VMEM((2, COLS), jnp.int32), pltpu.SemaphoreType.DMA((4,))],
        compiler_params=pltpu.CompilerParams(vmem_limit_bytes=4 * 2**20),
    )(blocks.reshape(2 * OBS, COLS), coef_first, coef_second, wet)
    shift = 4 * lax.axis_index("xh") + lax.axis_index("yh")
    shift = shift.astype(jnp.int32).reshape(1)
    own, shift = lax.optimization_barrier((own, shift))
    count = lax.axis_size(TILE)
    up = lax.ppermute(own, TILE, [(i, i + 1) for i in range(count - 1)])
    down = lax.ppermute(own, TILE, [(i + 1, i) for i in range(count - 1)])
    spread = call(smooth_body, (LAGS, OBS, COLS), (own, up, down))
    every = lax.all_to_all(spread, TM, 0, 0, tiled=True)
    part = call(
        lag_body,
        (2 * QUAD, OBS * OBS // QUAD // 128, 128),
        (every, shift),
        [
            pltpu.VMEM((LAGS, OBS, 2 * COLS), jnp.bfloat16),
            pltpu.VMEM((LAGS, OBS, 2 * COLS), jnp.bfloat16),
            pltpu.VMEM((OBS, OBS), jnp.float32),
        ],
        smem=1,
    )
    part = lax.all_to_all(part, ("xl", "yl", "c"), 0, 0, tiled=True)
    part = call(quad_body, (DEPTH, 16, 128), (part,))
    part = lax.all_to_all(part, "z", 0, 0, tiled=True)
    return call(final_body, (MINE, 1, OBS), (part,)).reshape(1, MINE, OBS)


def solution(mesh):
    finer = Mesh(mesh.devices.reshape(2, 2, 2, 16, 2, 2), TM + TILE)
    in_specs = (P(TM, None, TILE, None), P(TILE, None), P(TILE, None), P(TILE, None))
    return jax.shard_map(
        shards, mesh=finer, in_specs=in_specs, out_specs=P(TM, TILE, None), check_vma=False
    )
```

```python
import jax
import jax.numpy as jnp
from jax import lax
from jax.experimental import pallas as pl
from jax.experimental.pallas import tpu as pltpu
from jax.sharding import Mesh
from jax.sharding import PartitionSpec as P

TM = ("xh", "xl", "yh")
TILE = ("z", "yl", "c")
LAGS, OBS, COLS = 8, 320, 128
DEPTH, QUAD = 16, 4
MINE = OBS // (DEPTH * QUAD)
PACKED = 648

VM = pl.BlockSpec(memory_space=pltpu.VMEM)


def call(body, shape, args, scratch=(), limit=16, smem=0):
    specs = [VM] * (len(args) - smem) + [pl.BlockSpec(memory_space=pltpu.SMEM)] * smem
    return pl.pallas_call(
        body,
        out_shape=jax.ShapeDtypeStruct(shape, jnp.float32),
        in_specs=specs,
        out_specs=VM,
        scratch_shapes=list(scratch),
        compiler_params=pltpu.CompilerParams(vmem_limit_bytes=limit * 2**20),
    )(*args)


def pack_body(block_ref, fields_ref, out_ref):
    wet = fields_ref[2:4, :]
    both = jnp.concatenate([wet] * 4, axis=0)
    for i in range(0, 2 * OBS, 8):
        out_ref[i : i + 8, :] = block_ref[i : i + 8, :] * both
    out_ref[2 * OBS :, :] = fields_ref[...]


def smooth_body(own_ref, near_ref, far_ref, core_ref, out_ref):
    @pl.when(core_ref[0] == 0)
    def _():
        smooth(own_ref, far_ref, near_ref, out_ref)

    @pl.when(core_ref[0] == 1)
    def _():
        smooth(own_ref, near_ref, far_ref, out_ref)


def smooth(own_ref, up_ref, down_ref, out_ref):
    lane = lax.broadcasted_iota(jnp.int32, (1, COLS), 1)
    fifth_l = jnp.where(lane > 0, 0.2, 0.0).astype(jnp.float32)
    fifth_r = jnp.where(lane < COLS - 1, 0.2, 0.0).astype(jnp.float32)

    def lateral(u):
        return pltpu.roll(u, 1, 1) * fifth_l + pltpu.roll(u, COLS - 1, 1) * fifth_r

    def row(ref, i):
        return ref[2 * OBS + i : 2 * OBS + i + 1, :]

    coef = [row(up_ref, 1), row(own_ref, 0), row(own_ref, 1), row(down_ref, 0)]
    wet = [row(up_ref, 3), row(own_ref, 2), row(own_ref, 3), row(down_ref, 2)]
    late = [row(own_ref, 4), row(own_ref, 5)]
    n = 32
    for o in range(0, OBS, n):
        rows = [
            ref[pl.ds(2 * o + r, n, 2), :]
            for ref in (up_ref, own_ref, down_ref)
            for r in (0, 1)
        ]
        first = []
        for i in range(4):
            mid = rows[i + 1]
            total = coef[i] * mid + 0.2 * (rows[i] + rows[i + 2]) + lateral(mid)
            first.append(total * wet[i])
        for r in range(2):
            mid = first[r + 1]
            value = late[r] * mid + 0.2 * (first[r] + first[r + 2]) + lateral(mid)
            for t in range(LAGS):
                if t // 2 % 2 == r:
                    out_ref[t, o : o + n, :] = value


def lag_body(all_ref, shift_ref, out_ref, hi_ref, lo_ref, acc_ref):
    for g in range(LAGS):
        full = all_ref[g]
        hi = full.astype(jnp.bfloat16)
        lo = (full - hi.astype(jnp.float32)).astype(jnp.bfloat16)
        before = (g + LAGS - 1) % LAGS
        for ref, value in ((hi_ref, hi), (lo_ref, lo)):
            ref[g, :, 0:COLS] = value
            ref[before, :, COLS : 2 * COLS] = value

    def product(a, b):
        return lax.dot_general(
            a, b, (((1,), (1,)), ((), ())), preferred_element_type=jnp.float32
        )

    total = None
    for g in range(0, LAGS, 2):
        hi, lo = hi_ref[g], lo_ref[g]
        right = []
        for pick in range(2):
            partner = lax.rem(shift_ref[0] + (2 * pick + g), LAGS)
            hi_p, lo_p = hi_ref[partner], lo_ref[partner]
            right.append(jnp.concatenate([hi_p, lo_p, hi_p], axis=1))
        term = product(jnp.concatenate([hi, hi, lo], axis=1), jnp.concatenate(right, axis=0))
        total = term if total is None else total + term
    acc_ref[0] = total[:, 0:OBS]
    acc_ref[1] = total[:, OBS : 2 * OBS]
    half = DEPTH // 2 * MINE
    for pick in range(2):
        for q in range(QUAD):
            to_q = pick * QUAD + q
            for z in range(DEPTH):
                src = slice((z * QUAD + q) * MINE, (z * QUAD + q + 1) * MINE)
                to = z * MINE
                out_ref[to_q, to : to + MINE, :] = acc_ref[pick, src, 0:128]
                out_ref[to_q, 2 * half + to : 2 * half + to + MINE, :] = acc_ref[pick, src, 128:256]
                to, side = (to % half) + 4 * half, (to // half) * 64
                out_ref[to_q, to : to + MINE, side : side + 64] = acc_ref[pick, src, 256:320]


def summed(parts):
    while len(parts) > 1:
        parts = [a + b for a, b in zip(parts[::2], parts[1::2])]
    return parts[0]


def quad_body(in_ref, out_ref):
    half = DEPTH // 2 * MINE
    total = summed([in_ref[i] for i in range(2 * QUAD)])
    left, mid, last = total[: 2 * half], total[2 * half : 4 * half], total[4 * half :]
    swapped = pltpu.roll(last, 64, 1)
    for z in range(DEPTH):
        to = z * MINE
        side = last if to < half else swapped
        for i in range(MINE):
            row = to + i
            out_ref[z, :, i * OBS : i * OBS + 128] = left[row : row + 1]
            out_ref[z, :, i * OBS + 128 : i * OBS + 256] = mid[row : row + 1]
            row = row % half
            out_ref[z, :, i * OBS + 256 : i * OBS + 320] = side[row : row + 1, 0:64]


def final_body(in_ref, out_ref):
    total = summed([in_ref[i] for i in range(DEPTH)]) * (1.0 / 16384.0)
    for i in range(MINE):
        out_ref[i] = total[:, i * OBS : (i + 1) * OBS]


def shards(blocks, coef_first, coef_second, wet):
    fields = (coef_first, wet, coef_second)
    fields = sum(
        jnp.pad(f, ((2 * i, 6 - 2 * i), (0, 0))).astype(jnp.float32) for i, f in enumerate(fields)
    )
    own = call(pack_body, (PACKED, COLS), (blocks.reshape(2 * OBS, COLS), fields), limit=4)
    shift = 4 * lax.axis_index("xh") + lax.axis_index("yh")
    shift = shift.astype(jnp.int32).reshape(1)
    core = lax.axis_index("c").astype(jnp.int32).reshape(1)
    own, shift, core = lax.optimization_barrier((own, shift, core))
    pairs = [(i, i + 1) for i in range(1, lax.axis_size(TILE) - 1, 2)]
    far = lax.ppermute(own, TILE, pairs + [(b, a) for a, b in pairs])
    near = lax.ppermute(own, "c", [(0, 1), (1, 0)])
    spread = call(smooth_body, (LAGS, OBS, COLS), (own, near, far, core), smem=1)
    every = lax.all_to_all(spread, TM, 0, 0, tiled=True)
    part = call(
        lag_body,
        (2 * QUAD, OBS * OBS // QUAD // 128, 128),
        (every, shift),
        [
            pltpu.VMEM((LAGS, OBS, 2 * COLS), jnp.bfloat16),
            pltpu.VMEM((LAGS, OBS, 2 * COLS), jnp.bfloat16),
            pltpu.VMEM((2, OBS, OBS), jnp.float32),
        ],
        smem=1,
    )
    part = lax.all_to_all(part, ("xl", "yl", "c"), 0, 0, tiled=True)
    part = call(quad_body, (DEPTH, 1, MINE * OBS), (part,))
    part = lax.all_to_all(part, "z", 0, 0, tiled=True)
    return call(final_body, (MINE, 1, OBS), (part,)).reshape(1, MINE, OBS)


def solution(mesh):
    finer = Mesh(mesh.devices.reshape(2, 2, 2, 16, 2, 2), TM + TILE)
    in_specs = (P(TM, None, TILE, None), P(TILE, None), P(TILE, None), P(TILE, None))
    return jax.shard_map(
        shards, mesh=finer, in_specs=in_specs, out_specs=P(TM, TILE, None), check_vma=False
    )
```

```python
import functools

import jax
import jax.numpy as jnp
from jax import lax
from jax.experimental import pallas as pl
from jax.experimental.pallas import tpu as pltpu
from jax.sharding import Mesh
from jax.sharding import PartitionSpec as P

TM = ("xh", "xl", "yh")
TILE = ("z", "yl", "c")
LAGS, OBS, COLS = 8, 320, 128
DEPTH, QUAD = 16, 4
MINE = OBS // (DEPTH * QUAD)
PACKED = 648
HALF = OBS // 2

VM = pl.BlockSpec(memory_space=pltpu.VMEM)


def call(body, shape, args, scratch=(), limit=16, smem=0):
    specs = [VM] * (len(args) - smem) + [pl.BlockSpec(memory_space=pltpu.SMEM)] * smem
    return pl.pallas_call(
        body,
        out_shape=jax.ShapeDtypeStruct(shape, jnp.float32),
        in_specs=specs,
        out_specs=VM,
        scratch_shapes=list(scratch),
        compiler_params=pltpu.CompilerParams(vmem_limit_bytes=limit * 2**20),
    )(*args)


def pack_body(block_ref, fields_ref, out_ref):
    wet = fields_ref[2:4, :]
    both = jnp.concatenate([wet] * 4, axis=0)
    for i in range(0, 2 * OBS, 8):
        out_ref[i : i + 8, :] = block_ref[i : i + 8, :] * both
    out_ref[2 * OBS :, :] = fields_ref[...]


def smooth_body(own_ref, near_ref, far_ref, core_ref, out_ref):
    @pl.when(core_ref[0] == 0)
    def _():
        smooth(own_ref, far_ref, near_ref, out_ref)

    @pl.when(core_ref[0] == 1)
    def _():
        smooth(own_ref, near_ref, far_ref, out_ref)


def smooth(own_ref, up_ref, down_ref, out_ref):
    lane = lax.broadcasted_iota(jnp.int32, (1, COLS), 1)
    fifth_l = jnp.where(lane > 0, 0.2, 0.0).astype(jnp.float32)
    fifth_r = jnp.where(lane < COLS - 1, 0.2, 0.0).astype(jnp.float32)

    def lateral(u):
        return pltpu.roll(u, 1, 1) * fifth_l + pltpu.roll(u, COLS - 1, 1) * fifth_r

    def row(ref, i):
        return ref[2 * OBS + i : 2 * OBS + i + 1, :]

    coef = [row(up_ref, 1), row(own_ref, 0), row(own_ref, 1), row(down_ref, 0)]
    wet = [row(up_ref, 3), row(own_ref, 2), row(own_ref, 3), row(down_ref, 2)]
    late = [row(own_ref, 4), row(own_ref, 5)]
    n = 32
    for o in range(0, OBS, n):
        rows = [
            ref[pl.ds(2 * o + r, n, 2), :]
            for ref in (up_ref, own_ref, down_ref)
            for r in (0, 1)
        ]
        first = []
        for i in range(4):
            mid = rows[i + 1]
            total = coef[i] * mid + 0.2 * (rows[i] + rows[i + 2]) + lateral(mid)
            first.append(total * wet[i])
        for r in range(2):
            mid = first[r + 1]
            value = late[r] * mid + 0.2 * (first[r] + first[r + 2]) + lateral(mid)
            for t in range(LAGS):
                if t // 2 % 2 == r:
                    out_ref[t, o : o + n, :] = value


def split_body(all_ref, shift_ref, core_ref, out_ref, hi_ref, lo_ref):
    for g in range(LAGS):
        full = all_ref[g]
        hi = full.astype(jnp.bfloat16)
        lo = (full - hi.astype(jnp.float32)).astype(jnp.bfloat16)
        before = (g + LAGS - 1) % LAGS
        for ref, value in ((hi_ref, hi), (lo_ref, lo)):
            ref[g, :, 0:COLS] = value
            ref[before, :, COLS : 2 * COLS] = value
    lag_rows(1 - core_ref[0], hi_ref, lo_ref, shift_ref, out_ref)


def lag_body(hi_ref, lo_ref, shift_ref, core_ref, out_ref):
    lag_rows(core_ref[0], hi_ref, lo_ref, shift_ref, out_ref)


def lag_rows(half, hi_ref, lo_ref, shift_ref, out_ref):
    rows = pl.ds(pl.multiple_of(half * HALF, HALF), HALF)
    total = None
    for g in range(0, LAGS, 2):
        hi, lo = hi_ref[g, rows, :], lo_ref[g, rows, :]
        right = []
        for pick in range(2):
            partner = lax.rem(shift_ref[0] + (2 * pick + g), LAGS)
            hi_p, lo_p = hi_ref[partner], lo_ref[partner]
            right.append(jnp.concatenate([hi_p, lo_p, hi_p], axis=1))
        term = lax.dot_general(
            jnp.concatenate([hi, hi, lo], axis=1),
            jnp.concatenate(right, axis=0),
            (((1,), (1,)), ((), ())),
            preferred_element_type=jnp.float32,
        )
        total = term if total is None else total + term
    out_ref[0] = total[:, 0:OBS]
    out_ref[1] = total[:, OBS : 2 * OBS]


def deal_body(mine_ref, other_ref, out_ref, acc_ref):
    acc_ref[...] = mine_ref[...] + other_ref[...]
    count = DEPTH // 2 * MINE
    for pick in range(2):
        for q in range(QUAD):
            for z in range(DEPTH // 2):
                src = slice((z * QUAD + q) * MINE, (z * QUAD + q + 1) * MINE)
                chunk, to = pick * QUAD + q, z * MINE
                out_ref[chunk, to : to + MINE, :] = acc_ref[pick, src, 0:128]
                out_ref[chunk, count + to : count + to + MINE, :] = acc_ref[pick, src, 128:256]
                to, side = 2 * count + to % (count // 2), to // (count // 2) * 64
                out_ref[chunk, to : to + MINE, side : side + 64] = acc_ref[pick, src, 256:320]


def summed(parts):
    while len(parts) > 1:
        parts = [a + b for a, b in zip(parts[::2], parts[1::2])]
    return parts[0]


def quad_body(in_ref, out_ref):
    count = DEPTH // 2 * MINE
    for c in range(2):
        total = summed([in_ref[i] for i in range(c, 2 * QUAD, 2)])
        left, mid, last = total[:count], total[count : 2 * count], total[2 * count :]
        swapped = pltpu.roll(last, 64, 1)
        for row in range(count):
            z, i = c * DEPTH // 2 + row // MINE, row % MINE
            side = last if row < count // 2 else swapped
            at = row % (count // 2)
            out_ref[z, :, i * OBS : i * OBS + 128] = left[row : row + 1]
            out_ref[z, :, i * OBS + 128 : i * OBS + 256] = mid[row : row + 1]
            out_ref[z, :, i * OBS + 256 : i * OBS + 320] = side[at : at + 1, 0:64]


def final_body(in_ref, out_ref):
    total = summed([in_ref[i] for i in range(DEPTH)]) * (1.0 / 16384.0)
    for i in range(MINE):
        out_ref[i] = total[:, i * OBS : (i + 1) * OBS]


def shards(blocks, coef_first, coef_second, wet):
    fields = (coef_first, wet, coef_second)
    fields = sum(
        jnp.pad(f, ((2 * i, 6 - 2 * i), (0, 0))).astype(jnp.float32) for i, f in enumerate(fields)
    )
    own = call(pack_body, (PACKED, COLS), (blocks.reshape(2 * OBS, COLS), fields), limit=4)
    shift = 4 * lax.axis_index("xh") + lax.axis_index("yh")
    shift = shift.astype(jnp.int32).reshape(1)
    core = lax.axis_index("c").astype(jnp.int32).reshape(1)
    own, shift, core = lax.optimization_barrier((own, shift, core))
    pairs = [(i, i + 1) for i in range(1, lax.axis_size(TILE) - 1, 2)]
    far = lax.ppermute(own, TILE, pairs + [(b, a) for a, b in pairs])
    near = lax.ppermute(own, "c", [(0, 1), (1, 0)])
    spread = call(smooth_body, (LAGS, OBS, COLS), (own, near, far, core), smem=1)
    every = lax.all_to_all(spread, TM, 0, 0, tiled=True)
    split = jax.ShapeDtypeStruct((LAGS, OBS, 2 * COLS), jnp.bfloat16)
    half = jax.ShapeDtypeStruct((2, HALF, OBS), jnp.float32)
    smem = pl.BlockSpec(memory_space=pltpu.SMEM)
    other, hi, lo = pl.pallas_call(
        split_body,
        out_shape=[half, split, split],
        in_specs=[VM, smem, smem],
        out_specs=[VM] * 3,
        compiler_params=pltpu.CompilerParams(vmem_limit_bytes=16 * 2**20),
    )(every, shift, core)
    other = lax.ppermute(other, "c", [(0, 1), (1, 0)])
    mine = call(lag_body, half.shape, (hi, lo, shift, core), smem=2)
    chunks = (2 * QUAD, HALF * OBS // QUAD // 128, 128)
    part = call(deal_body, chunks, (mine, other), [pltpu.VMEM(half.shape, jnp.float32)])
    part = lax.all_to_all(part, ("xl", "yl", "c"), 0, 0, tiled=True)
    part = call(quad_body, (DEPTH, 1, MINE * OBS), (part,))
    part = lax.all_to_all(part, "z", 0, 0, tiled=True)
    return call(final_body, (MINE, 1, OBS), (part,)).reshape(1, MINE, OBS)


def solution(mesh):
    finer = Mesh(mesh.devices.reshape(2, 2, 2, 16, 2, 2), TM + TILE)
    in_specs = (P(TM, None, TILE, None), P(TILE, None), P(TILE, None), P(TILE, None))
    return jax.shard_map(
        shards, mesh=finer, in_specs=in_specs, out_specs=P(TM, TILE, None), check_vma=False
    )
```

```python
import functools

import jax
import jax.numpy as jnp
from jax import lax
from jax.experimental import pallas as pl
from jax.experimental.pallas import tpu as pltpu
from jax.sharding import Mesh
from jax.sharding import PartitionSpec as P

TM = ("xh", "xl", "yh")
TILE = ("z", "yl", "c")
LAGS, OBS, COLS = 8, 320, 128
DEPTH, QUAD = 16, 4
MINE = OBS // (DEPTH * QUAD)
PACKED = 648
HALF = OBS // 2

VM = pl.BlockSpec(memory_space=pltpu.VMEM)


def call(body, shape, args, scratch=(), limit=16, smem=0):
    specs = [VM] * (len(args) - smem) + [pl.BlockSpec(memory_space=pltpu.SMEM)] * smem
    return pl.pallas_call(
        body,
        out_shape=jax.ShapeDtypeStruct(shape, jnp.float32),
        in_specs=specs,
        out_specs=VM,
        scratch_shapes=list(scratch),
        compiler_params=pltpu.CompilerParams(vmem_limit_bytes=limit * 2**20),
    )(*args)


def pack_body(block_ref, fields_ref, out_ref):
    wet = fields_ref[2:4, :]
    both = jnp.concatenate([wet] * 4, axis=0)
    for i in range(0, 2 * OBS, 8):
        out_ref[i : i + 8, :] = block_ref[i : i + 8, :] * both
    out_ref[2 * OBS :, :] = fields_ref[...]


def smooth_body(own_ref, near_ref, far_ref, core_ref, out_ref):
    @pl.when(core_ref[0] == 0)
    def _():
        smooth(own_ref, far_ref, near_ref, out_ref)

    @pl.when(core_ref[0] == 1)
    def _():
        smooth(own_ref, near_ref, far_ref, out_ref)


def smooth(own_ref, up_ref, down_ref, out_ref):
    lane = lax.broadcasted_iota(jnp.int32, (1, COLS), 1)
    fifth_l = jnp.where(lane > 0, 0.2, 0.0).astype(jnp.float32)
    fifth_r = jnp.where(lane < COLS - 1, 0.2, 0.0).astype(jnp.float32)

    def lateral(u):
        return pltpu.roll(u, 1, 1) * fifth_l + pltpu.roll(u, COLS - 1, 1) * fifth_r

    def row(ref, i):
        return ref[2 * OBS + i : 2 * OBS + i + 1, :]

    coef = [row(up_ref, 1), row(own_ref, 0), row(own_ref, 1), row(down_ref, 0)]
    wet = [row(up_ref, 3), row(own_ref, 2), row(own_ref, 3), row(down_ref, 2)]
    late = [row(own_ref, 4), row(own_ref, 5)]
    n = 160
    for o in range(0, OBS, n):
        rows = [
            ref[pl.ds(2 * o + r, n, 2), :]
            for ref in (up_ref, own_ref, down_ref)
            for r in (0, 1)
        ]
        first = []
        for i in range(4):
            mid = rows[i + 1]
            total = coef[i] * mid + 0.2 * (rows[i] + rows[i + 2]) + lateral(mid)
            first.append(total * wet[i])
        for r in range(2):
            mid = first[r + 1]
            value = late[r] * mid + 0.2 * (first[r] + first[r + 2]) + lateral(mid)
            for t in range(LAGS):
                if t // 2 % 2 == r:
                    out_ref[t, o : o + n, :] = value


def split_body(all_ref, shift_ref, core_ref, out_ref, hi_ref, lo_ref):
    for g in range(LAGS):
        full = all_ref[g]
        hi = full.astype(jnp.bfloat16)
        lo = (full - hi.astype(jnp.float32)).astype(jnp.bfloat16)
        hi_ref[g], lo_ref[g] = hi, lo
    lag_whole(1 - core_ref[0], hi_ref, lo_ref, shift_ref, out_ref)


def lag_body(hi_ref, lo_ref, shift_ref, core_ref, out_ref):
    lag_rows(core_ref[0], hi_ref, lo_ref, shift_ref, out_ref)


def lag_rows(half, hi_ref, lo_ref, shift_ref, out_ref):
    rows = pl.ds(pl.multiple_of(half * HALF, HALF), HALF)
    total = None
    for g in range(0, LAGS, 2):
        left = [(hi_ref[i, rows, :], lo_ref[i, rows, :]) for i in (g, g + 1)]
        hi, lo = (jnp.concatenate(pair, axis=1) for pair in zip(*left))
        right = []
        for pick in range(2):
            at = [lax.rem(shift_ref[0] + (2 * pick + i), LAGS) for i in (g, g + 1)]
            hi_p, lo_p = (jnp.concatenate([ref[i] for i in at], axis=1) for ref in (hi_ref, lo_ref))
            right.append(jnp.concatenate([hi_p, lo_p, hi_p], axis=1))
        term = lax.dot_general(
            jnp.concatenate([hi, hi, lo], axis=1),
            jnp.concatenate(right, axis=0),
            (((1,), (1,)), ((), ())),
            preferred_element_type=jnp.float32,
        )
        total = term if total is None else total + term
    out_ref[0] = total[:, 0:OBS]
    out_ref[1] = total[:, OBS : 2 * OBS]


def lag_whole(half, hi_ref, lo_ref, shift_ref, out_ref):
    rows = pl.ds(pl.multiple_of(half * HALF, HALF), HALF)
    hi, lo = (jnp.concatenate([ref[g, rows, :] for g in range(LAGS)], axis=1) for ref in (hi_ref, lo_ref))
    right = []
    for pick in range(2):
        at = [lax.rem(shift_ref[0] + (2 * pick + g), LAGS) for g in range(LAGS)]
        hi_p, lo_p = (jnp.concatenate([ref[i] for i in at], axis=1) for ref in (hi_ref, lo_ref))
        right.append(jnp.concatenate([hi_p, lo_p, hi_p], axis=1))
    total = lax.dot_general(
        jnp.concatenate([hi, hi, lo], axis=1),
        jnp.concatenate(right, axis=0),
        (((1,), (1,)), ((), ())),
        preferred_element_type=jnp.float32,
    )
    out_ref[0] = total[:, 0:OBS]
    out_ref[1] = total[:, OBS : 2 * OBS]


def deal_body(mine_ref, other_ref, out_ref, acc_ref):
    acc_ref[...] = mine_ref[...] + other_ref[...]
    count = DEPTH // 2 * MINE
    for pick in range(2):
        for q in range(QUAD):
            for z in range(DEPTH // 2):
                src = slice((z * QUAD + q) * MINE, (z * QUAD + q + 1) * MINE)
                chunk, to = pick * QUAD + q, z * MINE
                out_ref[chunk, to : to + MINE, :] = acc_ref[pick, src, 0:128]
                out_ref[chunk, count + to : count + to + MINE, :] = acc_ref[pick, src, 128:256]
                to, side = 2 * count + to % (count // 2), to // (count // 2) * 64
                out_ref[chunk, to : to + MINE, side : side + 64] = acc_ref[pick, src, 256:320]


def summed(parts):
    while len(parts) > 1:
        parts = [a + b for a, b in zip(parts[::2], parts[1::2])]
    return parts[0]


def quad_body(in_ref, out_ref):
    count = DEPTH // 2 * MINE
    for c in range(2):
        total = summed([in_ref[i] for i in range(c, 2 * QUAD, 2)])
        left, mid, last = total[:count], total[count : 2 * count], total[2 * count :]
        swapped = pltpu.roll(last, 64, 1)
        for row in range(count):
            z, i = c * DEPTH // 2 + row // MINE, row % MINE
            side = last if row < count // 2 else swapped
            at = row % (count // 2)
            out_ref[z, :, i * OBS : i * OBS + 128] = left[row : row + 1]
            out_ref[z, :, i * OBS + 128 : i * OBS + 256] = mid[row : row + 1]
            out_ref[z, :, i * OBS + 256 : i * OBS + 320] = side[at : at + 1, 0:64]


def final_body(in_ref, out_ref):
    total = summed([in_ref[i] for i in range(DEPTH)]) * (1.0 / 16384.0)
    for i in range(MINE):
        out_ref[i] = total[:, i * OBS : (i + 1) * OBS]


def shards(blocks, coef_first, coef_second, wet):
    fields = (coef_first, wet, coef_second)
    fields = sum(
        jnp.pad(f, ((2 * i, 6 - 2 * i), (0, 0))).astype(jnp.float32) for i, f in enumerate(fields)
    )
    own = call(pack_body, (PACKED, COLS), (blocks.reshape(2 * OBS, COLS), fields), limit=4)
    shift = 4 * lax.axis_index("xh") + lax.axis_index("yh")
    shift = shift.astype(jnp.int32).reshape(1)
    core = lax.axis_index("c").astype(jnp.int32).reshape(1)
    own, shift, core = lax.optimization_barrier((own, shift, core))
    pairs = [(i, i + 1) for i in range(1, lax.axis_size(TILE) - 1, 2)]
    far = lax.ppermute(own, TILE, pairs + [(b, a) for a, b in pairs])
    near = lax.ppermute(own, "c", [(0, 1), (1, 0)])
    spread = call(smooth_body, (LAGS, OBS, COLS), (own, near, far, core), smem=1)
    every = lax.all_to_all(spread, TM, 0, 0, tiled=True)
    split = jax.ShapeDtypeStruct((LAGS, OBS, COLS), jnp.bfloat16)
    half = jax.ShapeDtypeStruct((2, HALF, OBS), jnp.float32)
    smem = pl.BlockSpec(memory_space=pltpu.SMEM)
    other, hi, lo = pl.pallas_call(
        split_body,
        out_shape=[half, split, split],
        in_specs=[VM, smem, smem],
        out_specs=[VM] * 3,
        compiler_params=pltpu.CompilerParams(vmem_limit_bytes=16 * 2**20),
    )(every, shift, core)
    other = lax.ppermute(other, "c", [(0, 1), (1, 0)])
    mine = call(lag_body, half.shape, (hi, lo, shift, core), smem=2)
    chunks = (2 * QUAD, HALF * OBS // QUAD // 128, 128)
    part = call(deal_body, chunks, (mine, other), [pltpu.VMEM(half.shape, jnp.float32)])
    part = lax.all_to_all(part, ("xl", "yl", "c"), 0, 0, tiled=True)
    part = call(quad_body, (DEPTH, 1, MINE * OBS), (part,))
    part = lax.all_to_all(part, "z", 0, 0, tiled=True)
    return call(final_body, (MINE, 1, OBS), (part,)).reshape(1, MINE, OBS)


def solution(mesh):
    finer = Mesh(mesh.devices.reshape(2, 2, 2, 16, 2, 2), TM + TILE)
    in_specs = (P(TM, None, TILE, None), P(TILE, None), P(TILE, None), P(TILE, None))
    return jax.shard_map(
        shards, mesh=finer, in_specs=in_specs, out_specs=P(TM, TILE, None), check_vma=False
    )
```

```python
import functools

import jax
import jax.numpy as jnp
from jax import lax
from jax.experimental import pallas as pl
from jax.experimental.pallas import tpu as pltpu
from jax.sharding import Mesh
from jax.sharding import PartitionSpec as P

TM = ("xh", "xl", "yh")
TILE = ("z", "yl", "c")
LAGS, OBS, COLS = 8, 320, 128
DEPTH, QUAD = 16, 4
MINE = OBS // (DEPTH * QUAD)
PACKED = 648
HALF = OBS // 2

VM = pl.BlockSpec(memory_space=pltpu.VMEM)


def call(body, shape, args, scratch=(), limit=16, smem=0):
    specs = [VM] * (len(args) - smem) + [pl.BlockSpec(memory_space=pltpu.SMEM)] * smem
    return pl.pallas_call(
        body,
        out_shape=jax.ShapeDtypeStruct(shape, jnp.float32),
        in_specs=specs,
        out_specs=VM,
        scratch_shapes=list(scratch),
        compiler_params=pltpu.CompilerParams(vmem_limit_bytes=limit * 2**20),
    )(*args)


def smooth_body(own_ref, near_ref, far_ref, core_ref, out_ref):
    @pl.when(core_ref[0] == 0)
    def _():
        smooth(own_ref, far_ref, near_ref, out_ref)

    @pl.when(core_ref[0] == 1)
    def _():
        smooth(own_ref, near_ref, far_ref, out_ref)


def smooth(own_ref, up_ref, down_ref, out_ref):
    lane = lax.broadcasted_iota(jnp.int32, (1, COLS), 1)
    fifth_l = jnp.where(lane > 0, 0.2, 0.0).astype(jnp.float32)
    fifth_r = jnp.where(lane < COLS - 1, 0.2, 0.0).astype(jnp.float32)

    def lateral(u):
        return pltpu.roll(u, 1, 1) * fifth_l + pltpu.roll(u, COLS - 1, 1) * fifth_r

    def row(ref, i):
        return ref[2 * OBS + i : 2 * OBS + i + 1, :]

    coef = [row(up_ref, 1), row(own_ref, 0), row(own_ref, 1), row(down_ref, 0)]
    wet = [row(ref, 2 + r) for ref in (up_ref, own_ref, down_ref) for r in (0, 1)]
    late = [row(own_ref, 4), row(own_ref, 5)]
    n = 160
    for o in range(0, OBS, n):
        rows = [
            ref[pl.ds(2 * o + r, n, 2), :] * wet[2 * i + r]
            for i, ref in enumerate((up_ref, own_ref, down_ref))
            for r in (0, 1)
        ]
        first = []
        for i in range(4):
            mid = rows[i + 1]
            total = coef[i] * mid + 0.2 * (rows[i] + rows[i + 2]) + lateral(mid)
            first.append(total * wet[i + 1])
        for r in range(2):
            mid = first[r + 1]
            value = late[r] * mid + 0.2 * (first[r] + first[r + 2]) + lateral(mid)
            for t in range(LAGS):
                if t // 2 % 2 == r:
                    out_ref[t, o : o + n, :] = value


def split_body(all_ref, shift_ref, core_ref, out_ref, hi_ref, lo_ref):
    for g in range(LAGS):
        full = all_ref[g]
        hi = full.astype(jnp.bfloat16)
        lo = (full - hi.astype(jnp.float32)).astype(jnp.bfloat16)
        hi_ref[g], lo_ref[g] = hi, lo
    lag_whole(1 - core_ref[0], hi_ref, lo_ref, shift_ref, out_ref)


def lag_body(hi_ref, lo_ref, shift_ref, core_ref, out_ref):
    lag_rows(core_ref[0], hi_ref, lo_ref, shift_ref, out_ref)


def lag_rows(half, hi_ref, lo_ref, shift_ref, out_ref):
    rows = pl.ds(pl.multiple_of(half * HALF, HALF), HALF)
    total = None
    for g in range(0, LAGS, 2):
        left = [(hi_ref[i, rows, :], lo_ref[i, rows, :]) for i in (g, g + 1)]
        hi, lo = (jnp.concatenate(pair, axis=1) for pair in zip(*left))
        right = []
        for pick in range(2):
            at = [lax.rem(shift_ref[0] + (2 * pick + i), LAGS) for i in (g, g + 1)]
            hi_p, lo_p = (jnp.concatenate([ref[i] for i in at], axis=1) for ref in (hi_ref, lo_ref))
            right.append(jnp.concatenate([hi_p, lo_p, hi_p], axis=1))
        term = lax.dot_general(
            jnp.concatenate([hi, hi, lo], axis=1),
            jnp.concatenate(right, axis=0),
            (((1,), (1,)), ((), ())),
            preferred_element_type=jnp.float32,
        )
        total = term if total is None else total + term
    out_ref[0] = total[:, 0:OBS]
    out_ref[1] = total[:, OBS : 2 * OBS]


def lag_whole(half, hi_ref, lo_ref, shift_ref, out_ref):
    rows = pl.ds(pl.multiple_of(half * HALF, HALF), HALF)
    hi, lo = (jnp.concatenate([ref[g, rows, :] for g in range(LAGS)], axis=1) for ref in (hi_ref, lo_ref))
    right = []
    for pick in range(2):
        at = [lax.rem(shift_ref[0] + (2 * pick + g), LAGS) for g in range(LAGS)]
        hi_p, lo_p = (jnp.concatenate([ref[i] for i in at], axis=1) for ref in (hi_ref, lo_ref))
        right.append(jnp.concatenate([hi_p, lo_p, hi_p], axis=1))
    total = lax.dot_general(
        jnp.concatenate([hi, hi, lo], axis=1),
        jnp.concatenate(right, axis=0),
        (((1,), (1,)), ((), ())),
        preferred_element_type=jnp.float32,
    )
    out_ref[0] = total[:, 0:OBS]
    out_ref[1] = total[:, OBS : 2 * OBS]


def deal_body(mine_ref, other_ref, out_ref, acc_ref):
    acc_ref[...] = mine_ref[...] + other_ref[...]
    count = DEPTH // 2 * MINE
    for pick in range(2):
        for q in range(QUAD):
            for z in range(DEPTH // 2):
                src = slice((z * QUAD + q) * MINE, (z * QUAD + q + 1) * MINE)
                chunk, to = pick * QUAD + q, z * MINE
                out_ref[chunk, to : to + MINE, :] = acc_ref[pick, src, 0:128]
                out_ref[chunk, count + to : count + to + MINE, :] = acc_ref[pick, src, 128:256]
                to, side = 2 * count + to % (count // 2), to // (count // 2) * 64
                out_ref[chunk, to : to + MINE, side : side + 64] = acc_ref[pick, src, 256:320]


def summed(parts):
    while len(parts) > 1:
        parts = [a + b for a, b in zip(parts[::2], parts[1::2])]
    return parts[0]


def quad_body(in_ref, out_ref):
    count = DEPTH // 2 * MINE
    for c in range(2):
        total = summed([in_ref[i] for i in range(c, 2 * QUAD, 2)])
        left, mid, last = total[:count], total[count : 2 * count], total[2 * count :]
        swapped = pltpu.roll(last, 64, 1)
        for row in range(count):
            z, i = c * DEPTH // 2 + row // MINE, row % MINE
            side = last if row < count // 2 else swapped
            at = row % (count // 2)
            out_ref[z, :, i * OBS : i * OBS + 128] = left[row : row + 1]
            out_ref[z, :, i * OBS + 128 : i * OBS + 256] = mid[row : row + 1]
            out_ref[z, :, i * OBS + 256 : i * OBS + 320] = side[at : at + 1, 0:64]


def final_body(in_ref, out_ref):
    total = summed([in_ref[i] for i in range(DEPTH)]) * (1.0 / 16384.0)
    for i in range(MINE):
        out_ref[i] = total[:, i * OBS : (i + 1) * OBS]


def shards(blocks, coef_first, coef_second, wet):
    own = jnp.pad(blocks[0], ((0, (PACKED - 2 * OBS) // 2), (0, 0), (0, 0)))
    for i, field in enumerate((coef_first, wet, coef_second)):
        room = ((OBS + i, 3 - i), (0, 0), (0, 0))
        own = own + jnp.pad(field[None], room).astype(jnp.float32)
    own = own.reshape(PACKED, COLS)
    shift = 4 * lax.axis_index("xh") + lax.axis_index("yh")
    shift = shift.astype(jnp.int32).reshape(1)
    core = lax.axis_index("c").astype(jnp.int32).reshape(1)
    own, shift, core = lax.optimization_barrier((own, shift, core))
    pairs = [(i, i + 1) for i in range(1, lax.axis_size(TILE) - 1, 2)]
    far = lax.ppermute(own, TILE, pairs + [(b, a) for a, b in pairs])
    near = lax.ppermute(own, "c", [(0, 1), (1, 0)])
    spread = call(smooth_body, (LAGS, OBS, COLS), (own, near, far, core), smem=1)
    every = lax.all_to_all(spread, TM, 0, 0, tiled=True)
    split = jax.ShapeDtypeStruct((LAGS, OBS, COLS), jnp.bfloat16)
    half = jax.ShapeDtypeStruct((2, HALF, OBS), jnp.float32)
    smem = pl.BlockSpec(memory_space=pltpu.SMEM)
    other, hi, lo = pl.pallas_call(
        split_body,
        out_shape=[half, split, split],
        in_specs=[VM, smem, smem],
        out_specs=[VM] * 3,
        compiler_params=pltpu.CompilerParams(vmem_limit_bytes=16 * 2**20),
    )(every, shift, core)
    other = lax.ppermute(other, "c", [(0, 1), (1, 0)])
    mine = call(lag_body, half.shape, (hi, lo, shift, core), smem=2)
    chunks = (2 * QUAD, HALF * OBS // QUAD // 128, 128)
    part = call(deal_body, chunks, (mine, other), [pltpu.VMEM(half.shape, jnp.float32)])
    part = lax.all_to_all(part, ("xl", "yl", "c"), 0, 0, tiled=True)
    part = call(quad_body, (DEPTH, 1, MINE * OBS), (part,))
    part = lax.all_to_all(part, "z", 0, 0, tiled=True)
    return call(final_body, (MINE, 1, OBS), (part,)).reshape(1, MINE, OBS)


def solution(mesh):
    finer = Mesh(mesh.devices.reshape(2, 2, 2, 16, 2, 2), TM + TILE)
    in_specs = (P(TM, None, TILE, None), P(TILE, None), P(TILE, None), P(TILE, None))
    return jax.shard_map(
        shards, mesh=finer, in_specs=in_specs, out_specs=P(TM, TILE, None), check_vma=False
    )
```
